1024 devices in a mesh: group: 32 (over z, core), member: 32 (over y, x).
Axes of the slice: x: 4, y: 8, z: 16, core: 2. Of those that a mesh axis runs over, the one named last changes fastest.
Arguments:
- source: float32 [1024, 1024, 128], P('group', 'member'), may hold values from -5 to 8
- potential: float32 [1024, 1024, 128], P('group', 'member'), may hold values from -3 to 3
- refined: int32 [32, 32, 4], P('group', 'member'), may hold values 0 or 1
Outputs:
- smoothed: float32 [1024, 1024, 128], P('group', 'member')
- residual: float32 [1024, 1024, 128], P('group', 'member')
The draws below stay inside these ranges and needn't reach their ends.
Inputs may be any that keep to these rules, and one draw needn't show every extreme that they name: 1 marks a refined box, 0 one that is not smoothed on the fine level.
All inputs are finite; a program needn't handle non-finite values. No bound on the sum of `refined` on one device may be relied on, other than what follows from the above.
Results may differ from the reference program's by a relative error of at most 0.000035.
Values sent between devices are 32-bit elements; how exact they have to be, the bound alone decides.
No kernel may reach another device: no remote copies, remote signals or barrier semaphores. Data moves between devices by JAX's collectives and lax.ppermute only.
A program may use at most 128 MiB of HBM per device.

```python
import jax
import jax.numpy as jnp
from jax import lax

BOX = 32
NZB = 4
PRE = 2
POST = 2
COARSE = 2
NX = 1024
NY = 1024
NZ = 128
N_GROUP = 32
N_MEMBER = 32


def draw_source(key, part):
    key_noise = jax.random.fold_in(key, 11)
    shape = (NX, NY, NZ)
    along_x = lax.broadcasted_iota(jnp.float32, shape, 0) / (NX - 1.0)
    along_y = lax.broadcasted_iota(jnp.float32, shape, 1) / (NY - 1.0)
    noise = jnp.clip(jax.random.normal(key_noise, shape, jnp.float32), -4.0, 4.0)
    offset = 1.0 + along_x + along_y
    return (noise + offset).astype(jnp.float32)


def set_ends(entries, key, smallest, high):
    shape = entries.shape
    index_at = [jax.random.randint(jax.random.fold_in(key, axis), (), 0, shape[axis]) for axis in range(len(shape))]
    entries = entries.at[tuple(index_at)].set(smallest)
    longest = shape.index(max(shape))
    index_at[longest] = (index_at[longest] + 1) % shape[longest]
    return entries.at[tuple(index_at)].set(high)


def levels(key, dims, pieces, low, high):
    def one(axis_at, parts):
        draws = jax.random.uniform(jax.random.fold_in(jax.random.fold_in(key, 6), axis_at), (parts,), jnp.float32, low / len(pieces), high / len(pieces))
        return jnp.repeat(jnp.exp(draws), dims[axis_at] // parts).reshape((-1,) + (1,) * (len(dims) - axis_at - 1))

    gain = one(*pieces[0])
    for cut in pieces[1:]:
        gain = gain * one(*cut)
    return gain


def normal_values(stream_key, dims, deviation, most, shards=(), held_as=jnp.bfloat16):
    array = deviation * jax.random.normal(stream_key, dims, jnp.float32)
    if shards:
        array = array * levels(stream_key, dims, shards, -0.22, 0.18)
    return jnp.clip(array, -most, most).astype(held_as)


def setup_inputs(seed: int = 0) -> dict:
    keys = jax.random.split(jax.random.key(seed), 4)
    source = draw_source(jax.random.fold_in(keys[3], 71), 0)
    potential = normal_values(keys[1], (NX, NY, NZ), 0.5, 3.0, ((0, 32), (1, 32)), jnp.float32)
    refined = set_ends((jax.random.randint(keys[2], (N_GROUP, N_MEMBER, NZB), 0, 4) < 3).astype(jnp.int32), jax.random.fold_in(keys[2], 1), 0, 1)
    return {"source": source, "potential": potential, "refined": refined}


def neighbour_sum(grid_field):
    padded = jnp.pad(grid_field, 1)
    total = padded[2:, 1:-1, 1:-1] + padded[:-2, 1:-1, 1:-1]
    total = total + padded[1:-1, 2:, 1:-1] + padded[1:-1, :-2, 1:-1]
    return total + padded[1:-1, 1:-1, 2:] + padded[1:-1, 1:-1, :-2]


def expand(values_in, factor):
    size_a, size_b, size_c = values_in.shape
    wide = jnp.broadcast_to(values_in[:, None, :, None, :, None], (size_a, factor, size_b, factor, size_c, factor))
    return wide.reshape(size_a * factor, size_b * factor, size_c * factor)


def parity_of(shape):
    along_x = lax.broadcasted_iota(jnp.int32, shape, 0)
    along_y = lax.broadcasted_iota(jnp.int32, shape, 1)
    along_z = lax.broadcasted_iota(jnp.int32, shape, 2)
    return (along_x + along_y + along_z) % 2


def red_black(grid_field, right_side, active, parity):
    for colour in (0, 1):
        update = (right_side + neighbour_sum(grid_field)) / 6.0
        grid_field = jnp.where((parity == colour) & active, update, grid_field)
    return grid_field


def reference(source, potential, refined):
    density_mean = jnp.sum(source) / (NX * NY * NZ)
    contrast = source - density_mean
    active = expand(refined == 1, BOX)
    parity = parity_of(source.shape)
    phi = potential
    for _ in range(PRE):
        phi = red_black(phi, contrast, active, parity)
    fine_residual = contrast - (6.0 * phi - neighbour_sum(phi))
    size_a, size_b, size_c = fine_residual.shape
    coarse_source = fine_residual.reshape(size_a // 2, 2, size_b // 2, 2, size_c // 2, 2).sum(axis=(1, 3, 5)) * 0.5
    coarse_parity = parity_of(coarse_source.shape)
    correction = jnp.zeros(coarse_source.shape, jnp.float32)
    for _ in range(COARSE):
        correction = red_black(correction, coarse_source, True, coarse_parity)
    phi = phi + expand(correction, 2)
    for _ in range(POST):
        phi = red_black(phi, contrast, active, parity)
    residual = contrast - (6.0 * phi - neighbour_sum(phi))
    return phi, residual
```

```python
import jax
import jax.numpy as jnp
from jax import lax
from jax.experimental import pallas as pl
from jax.experimental.pallas import tpu as pltpu
from jax.sharding import PartitionSpec as P

GROUP = "group"
MEMBER = "member"
N = 32
NZ = 128
K = N // 2
H = 16
KH = H // 2
NX = N + 2 * H
NK = K + 2 * KH
PAD = 8
SIXTH = 1.0 / 6.0
F32 = jnp.float32
LIMIT = 40 * 1024 * 1024


def lanes(rows):
    return lax.broadcasted_iota(jnp.int32, (rows, NZ), 1)


def rows_of(rows):
    return lax.broadcasted_iota(jnp.int32, (rows, NZ), 0)


def split(ref, x, first):
    even = ref[x, pl.ds(0, K, stride=2), :]
    odd = ref[x, pl.ds(1, K, stride=2), :]
    return jnp.where(first, even, odd), jnp.where(first, odd, even)


def box_flags(refined, rows):
    z = lanes(rows)
    out = jnp.zeros((rows, NZ), F32)
    for b in range(NZ // N):
        on = jnp.where(refined[0, 0, b] == 1, 1.0, 0.0).astype(F32)
        out = jnp.where(z // N == b, on, out)
    return out


def pack_kernel(source, potential, refined, up, down, part):
    zp = lanes(K) % 2
    row = rows_of(8)
    zp8 = lanes(8) % 2

    def body(i, acc):
        for j in range(2):
            x = 2 * i + j
            first = zp == j
            pr, pb = split(potential, x, first)
            sr, sb = split(source, x, first)
            acc = acc + (sr + sb)
            up[x] = pr[KH:]
            down[x] = pr[:KH]
            up[N + x] = pb[KH:]
            down[N + x] = pb[:KH]
            beyond_up = jnp.where((row == 0) & (zp8 == j), pltpu.roll(pb[:KH], 1, 0), 0.0)
            beyond_down = jnp.where((row == KH - 1) & (zp8 != j), pltpu.roll(pb[KH:], KH - 1, 0), 0.0)
            up[2 * N + x] = sr[KH:] + beyond_up
            down[2 * N + x] = sr[:KH] + beyond_down
            up[3 * N + x] = sb[KH:]
            down[3 * N + x] = sb[:KH]
        return acc

    acc = lax.fori_loop(0, N // 2, body, jnp.zeros((K, NZ), F32))
    part[...] = jnp.broadcast_to(jnp.sum(acc, axis=0, keepdims=True), part.shape)
    flags = box_flags(refined, 8)
    up[4 * N] = flags
    down[4 * N] = flags


def middle_kernel(source, potential, refined, low, high, parts, up, down, wide, part):
    zp = lanes(K) % 2

    def put(ref, at, x, a, own):
        ref[at, :KH] = low[a * N + x]
        ref[at, KH : KH + K] = own
        ref[at, KH + K :] = high[a * N + x]

    for half, msg in ((0, down), (1, up)):

        def body(i, carry, half=half, msg=msg):
            for j in range(2):
                xh = 2 * i + j
                x = xh + half * H
                first = zp == j
                fields = split(potential, x, first) + split(source, x, first)
                for a in range(4):
                    put(wide, a * N + x, x, a, fields[a])
                    put(msg, a * H + xh, x, a, fields[a])
            return carry

        lax.fori_loop(0, H // 2, body, 0)
    up[2 * H] = up[2 * H] + wide[N + H - 1]
    down[3 * H - 1] = down[3 * H - 1] + wide[N + H]
    flags = box_flags(refined, K)
    for ref, at in ((up, 4 * H), (down, 4 * H), (wide, 4 * N)):
        ref[at, :KH] = low[4 * N]
        ref[at, KH : KH + K] = flags
        ref[at, KH + K :] = high[4 * N]
    part[...] = jnp.broadcast_to(jnp.sum(parts[...], axis=0, keepdims=True), part.shape)


def neighbours(ref, x, r0, rows, here, below_first, z):
    centre = ref[x, r0 : r0 + rows, :]
    below = ref[x, r0 - 1 : r0 - 1 + rows, :]
    above = ref[x, r0 + 1 : r0 + 1 + rows, :]
    side = jnp.where(here, below, above) if below_first else jnp.where(here, above, below)
    left = jnp.where(z == 0, 0.0, pltpu.roll(centre, 1, 1))
    right = jnp.where(z == NZ - 1, 0.0, pltpu.roll(centre, NZ - 1, 1))
    along_x = ref[x - 1, r0 : r0 + rows, :] + ref[x + 1, r0 : r0 + rows, :]
    return (along_x + (centre + side)) + (left + right)


def half_sweep(dst, src, rhs, masks, colour, x_from, x_to, row_from, rows):
    z = lanes(rows)
    zp = z % 2
    r0 = PAD + row_from

    def body(i, carry):
        base = x_from + 4 * i
        on = masks[base // H, row_from : row_from + rows, :] > 0.5
        for j in range(4):
            x = base + j
            total = neighbours(src, x + 1, r0, rows, zp == j % 2, colour == 0, z)
            update = rhs[x, row_from : row_from + rows, :] + total * SIXTH
            dst[x + 1, r0 : r0 + rows, :] = jnp.where(on, update, dst[x + 1, r0 : r0 + rows, :])
        return carry

    lax.fori_loop(0, (x_to - x_from) // 4, body, 0)


def cycle_kernel(wide, low, high, parts, place, smoothed, residual, red, black, rhs_r, rhs_b, masks, coarse, corr):
    cells = place[2] * place[3] * (N * N * NZ)
    mean = jnp.sum(parts[...]) / cells.astype(F32)

    spare = jnp.zeros((PAD, NZ), F32)
    for ref in (red, black):
        for x in (0, NX + 1):
            ref[x] = jnp.zeros((NK + 2 * PAD, NZ), F32)
    for part, start, count in ((low, 0, H), (wide, H, N), (high, H + N, H)):

        def body(i, carry, part=part, start=start, count=count):
            x = start + i
            for a, ref in ((0, red), (1, black)):
                ref[x + 1, :PAD, :] = spare
                ref[x + 1, PAD : PAD + NK, :] = part[a * count + i]
                ref[x + 1, PAD + NK :, :] = spare
            rhs_r[x] = (part[2 * count + i] - mean) * SIXTH
            rhs_b[x] = (part[3 * count + i] - mean) * SIXTH
            return carry

        lax.fori_loop(0, count, body, 0, unroll=2)
    masks[0] = low[4 * H]
    masks[1] = wide[4 * N]
    masks[2] = wide[4 * N]
    masks[3] = high[4 * H]

    for _ in range(2):
        half_sweep(red, black, rhs_r, masks, 0, 0, NX, 0, NK)
        half_sweep(black, red, rhs_b, masks, 1, 0, NX, 0, NK)

    z = lanes(NK)
    zp = z % 2

    def restrict(cx, carry):
        total = jnp.zeros((NK, NZ), F32)
        for j in range(2):
            x = 2 * cx + j
            here = zp == j
            r = slice(PAD, PAD + NK)
            nr = neighbours(black, x + 1, PAD, NK, here, True, z)
            nb = neighbours(red, x + 1, PAD, NK, here, False, z)
            gap = (rhs_r[x] - red[x + 1, r, :]) + (rhs_b[x] - black[x + 1, r, :])
            total = total + (6.0 * gap + (nr + nb))
        pair = jnp.where(zp == 0, pltpu.roll(total, NZ - 1, 1), pltpu.roll(total, 1, 1))
        coarse[cx] = (total + pair) * 0.5
        return carry

    lax.fori_loop(2, NX // 2 - 2, restrict, 0)

    row = rows_of(NK)
    global_row = place[1] * K + row - KH
    row_gain = jnp.where((global_row >= 0) & (global_row < place[3] * K), SIXTH, 0.0).astype(F32)
    parity = (row + z // 2) % 2
    for x in (0, 1, NX // 2 - 2, NX // 2 - 1):
        corr[x] = jnp.zeros((NK + 2 * PAD, NZ), F32)

    def gain_at(cx):
        at = place[0] * K + cx - KH
        return row_gain * jnp.where((at >= 0) & (at < place[2] * K), 1.0, 0.0).astype(F32)

    def start(i, carry):
        for j in range(2):
            cx = 2 * i + j
            corr[cx, :PAD, :] = spare
            corr[cx, PAD : PAD + NK, :] = jnp.where(parity == j, coarse[cx] * gain_at(cx), 0.0)
            corr[cx, PAD + NK :, :] = spare
        return carry

    lax.fori_loop(1, NX // 4 - 1, start, 0)

    def coarse_half(colour, first, last):
        def body(i, carry):
            for j in range(2):
                cx = 2 * i + j
                centre = corr[cx, PAD : PAD + NK, :]
                along_y = corr[cx, PAD - 1 : PAD - 1 + NK, :] + corr[cx, PAD + 1 : PAD + 1 + NK, :]
                along_x = corr[cx - 1, PAD : PAD + NK, :] + corr[cx + 1, PAD : PAD + NK, :]
                left = jnp.where(z < 2, 0.0, pltpu.roll(centre, 2, 1))
                right = jnp.where(z >= NZ - 2, 0.0, pltpu.roll(centre, NZ - 2, 1))
                update = (coarse[cx] + (along_x + along_y) + (left + right)) * gain_at(cx)
                corr[cx, PAD : PAD + NK, :] = jnp.where(parity == (colour + j) % 2, update, centre)
            return carry

        lax.fori_loop(first // 2, last // 2, body, 0)

    coarse_half(1, 2, 30)
    coarse_half(0, 4, 28)
    coarse_half(1, 4, 28)

    def prolong(cx, carry):
        add = corr[cx, PAD : PAD + NK, :]
        for ref in (red, black):
            for j in range(2):
                x = 2 * cx + j + 1
                ref[x, PAD : PAD + NK, :] = ref[x, PAD : PAD + NK, :] + add
        return carry

    lax.fori_loop(5, 27, prolong, 0)

    for _ in range(2):
        half_sweep(red, black, rhs_r, masks, 0, 12, 52, 4, 24)
        half_sweep(black, red, rhs_b, masks, 1, 12, 52, 4, 24)

    zk = lanes(K)
    zkp = zk % 2
    r0 = PAD + KH

    def finish(i, carry):
        for j in range(2):
            out = 2 * i + j
            x = out + H
            here = zkp == j
            r = red[x + 1, r0 : r0 + K, :]
            b = black[x + 1, r0 : r0 + K, :]
            res_r = 6.0 * (rhs_r[x, KH : KH + K, :] - r) + neighbours(black, x + 1, r0, K, here, True, zk)
            res_b = 6.0 * (rhs_b[x, KH : KH + K, :] - b) + neighbours(red, x + 1, r0, K, here, False, zk)
            for ref, one, two in ((smoothed, r, b), (residual, res_r, res_b)):
                ref[out, pl.ds(0, K, stride=2), :] = jnp.where(here, one, two)
                ref[out, pl.ds(1, K, stride=2), :] = jnp.where(here, two, one)
        return carry

    lax.fori_loop(0, N // 2, finish, 0)


def shape(*dims):
    return jax.ShapeDtypeStruct(dims, F32)


VMEM = pl.BlockSpec(memory_space=pltpu.VMEM)
SMEM = pl.BlockSpec(memory_space=pltpu.SMEM)


def call(kernel, ins, outs, scratch=()):
    return pl.pallas_call(
        kernel,
        out_shape=outs,
        in_specs=ins,
        out_specs=[VMEM] * len(outs),
        scratch_shapes=list(scratch),
        compiler_params=pltpu.CompilerParams(vmem_limit_bytes=LIMIT),
    )


def per_device(source, potential, refined):
    groups, members = lax.axis_size(GROUP), lax.axis_size(MEMBER)

    def both_ways(up, down, axis):
        size = lax.axis_size(axis)
        pairs = [(i, i + 1) for i in range(size - 1)]
        return lax.ppermute(up, axis, pairs), lax.ppermute(down, axis, [(b, a) for a, b in pairs])

    side = shape(4 * N + 1, KH, NZ)
    up, down, part = call(pack_kernel, [VMEM, VMEM, SMEM], [side, side, shape(groups, NZ)])(
        source, potential, refined
    )
    low, high = both_ways(up, down, MEMBER)
    parts = lax.all_to_all(part, GROUP, 0, 0, tiled=True)
    slab = shape(4 * H + 1, NK, NZ)
    up, down, wide, part = call(
        middle_kernel,
        [VMEM, VMEM, SMEM, VMEM, VMEM, VMEM],
        [slab, slab, shape(4 * N + 1, NK, NZ), shape(members, NZ)],
    )(source, potential, refined, low, high, parts)
    low, high = both_ways(up, down, GROUP)
    parts = lax.all_to_all(part, MEMBER, 0, 0, tiled=True)
    place = jnp.stack(
        [lax.axis_index(GROUP), lax.axis_index(MEMBER), jnp.int32(groups), jnp.int32(members)]
    ).astype(jnp.int32)
    padded = pltpu.VMEM((NX + 2, NK + 2 * PAD, NZ), F32)
    plain = pltpu.VMEM((NX, NK, NZ), F32)
    return call(
        cycle_kernel,
        [VMEM, VMEM, VMEM, VMEM, SMEM],
        [shape(N, N, NZ), shape(N, N, NZ)],
        [
            padded,
            padded,
            plain,
            plain,
            pltpu.VMEM((4, NK, NZ), F32),
            pltpu.VMEM((NX // 2, NK, NZ), F32),
            pltpu.VMEM((NX // 2, NK + 2 * PAD, NZ), F32),
        ],
    )(wide, low, high, parts, place)


def solution(mesh):
    spec = P(GROUP, MEMBER, None)
    return jax.shard_map(
        per_device, mesh=mesh, in_specs=(spec, spec, spec), out_specs=(spec, spec), check_vma=False
    )
```

```python
import jax
import jax.numpy as jnp
from jax import lax
from jax.experimental import pallas as pl
from jax.experimental.pallas import tpu as pltpu
from jax.sharding import PartitionSpec as P

GROUP = "group"
MEMBER = "member"
N = 32
NZ = 128
K = N // 2
H = 16
KH = H // 2
NX = N + 2 * H
NK = K + 2 * KH
NC = NX // 2
PAD = 8
SIXTH = 1.0 / 6.0
F32 = jnp.float32
MIB = 1024 * 1024
CHUNKS = 1
EXTRA, FLAGS = 4 * H, 4 * H + 1
SEGMENT = 4 * H + 2


def lanes(rows):
    return lax.broadcasted_iota(jnp.int32, (rows, NZ), 1)


def rows_of(rows):
    return lax.broadcasted_iota(jnp.int32, (rows, NZ), 0)


def split(ref, x, first):
    even = ref[x, pl.ds(0, K, stride=2), :]
    odd = ref[x, pl.ds(1, K, stride=2), :]
    return jnp.where(first, even, odd), jnp.where(first, odd, even)


def pack_kernel(source_any, potential_any, refined_any, up, down, part, own_flags, source, potential, refined, sems):
    size = N // CHUNKS
    flag_copy = pltpu.make_async_copy(refined_any, refined, sems.at[2 * CHUNKS])
    flag_copy.start()
    copies = []
    for c in range(CHUNKS):
        planes = pl.ds(c * size, size)
        pair = []
        for a, (src, dst) in enumerate(((source_any, source), (potential_any, potential))):
            pair.append(pltpu.make_async_copy(src.at[planes], dst.at[planes], sems.at[2 * c + a]))
        for copy in pair:
            copy.start()
        copies.append(pair)
    zp = lanes(K) % 2
    row = rows_of(KH)
    zp8 = lanes(KH) % 2
    acc = [jnp.zeros((K, NZ), F32), jnp.zeros((K, NZ), F32)]
    for x in range(N):
        if x % size == 0:
            for copy in copies[x // size]:
                copy.wait()
        j = x % 2
        first = zp == j
        pr, pb = split(potential, x, first)
        sr, sb = split(source, x, first)
        acc[j] = acc[j] + (sr + sb)
        up[x] = pr[KH:]
        down[x] = pr[:KH]
        up[N + x] = pb[KH:]
        down[N + x] = pb[:KH]
        beyond_up = jnp.where((row == 0) & (zp8 == j), pltpu.roll(pb[:KH], 1, 0), 0.0)
        beyond_down = jnp.where((row == KH - 1) & (zp8 != j), pltpu.roll(pb[KH:], KH - 1, 0), 0.0)
        up[2 * N + x] = sr[KH:] + beyond_up
        down[2 * N + x] = sr[:KH] + beyond_down
        up[3 * N + x] = sb[KH:]
        down[3 * N + x] = sb[:KH]
    total = jnp.sum(acc[0] + acc[1], axis=0, keepdims=True)
    part[...] = jnp.broadcast_to(total, part.shape)
    flag_copy.wait()
    box = lanes(KH) // N
    flags = jnp.zeros((KH, NZ), F32)
    for b in range(NZ // N):
        on = jnp.where(refined[0, 0, b] == 1, 1.0, 0.0).astype(F32)
        flags = jnp.where(box == b, on, flags)
    for ref in (up, down):
        ref[4 * N] = flags
    own_flags[...] = flags


def middle_kernel(source, potential, flags, low, high, parts, first_half, second_half, part, own, sem):
    copy = pltpu.make_async_copy(flags, own, sem)
    copy.start()
    zp = lanes(K) % 2
    for x in range(N):
        ref, at = (first_half, x) if x < H else (second_half, x - H)
        here = zp == x % 2
        fields = split(potential, x, here) + split(source, x, here)
        for a in range(4):
            ref[a * H + at, :KH] = low[a * N + x]
            ref[a * H + at, KH : KH + K] = fields[a]
            ref[a * H + at, KH + K :] = high[a * N + x]
            if a == 1 and x in (H - 1, H):
                far = second_half if x == H - 1 else first_half
                far[EXTRA, :KH] = low[a * N + x]
                far[EXTRA, KH : KH + K] = fields[a]
                far[EXTRA, KH + K :] = high[a * N + x]
    copy.wait()
    for ref in (first_half, second_half):
        ref[FLAGS, :KH] = low[4 * N]
        ref[FLAGS, KH : 2 * KH] = own[...]
        ref[FLAGS, 2 * KH : 3 * KH] = own[...]
        ref[FLAGS, 3 * KH :] = high[4 * N]
    part[...] = jnp.broadcast_to(jnp.sum(parts[...], axis=0, keepdims=True), part.shape)


def lane_sum(values, step, z):
    left = jnp.where(z < step, 0.0, pltpu.roll(values, step, 1))
    right = jnp.where(z >= NZ - step, 0.0, pltpu.roll(values, NZ - step, 1))
    return left + right


def cycle_kernel(seg0, seg1, seg2, seg3, parts, place, smoothed, residual, red, black, coarse, corr):
    segments = (seg0, seg1, seg2, seg3)
    cells = place[2] * place[3] * (N * N * NZ)
    mean = jnp.sum(parts[...]) / cells.astype(F32)

    def field(a, x, rows=slice(None)):
        return segments[x // H][a * H + x % H, rows, :]

    def right_side(colour, x, rows=slice(None)):
        return field(2 + colour, x, rows) - mean

    def sides(ref, x, r0, rows, colour, zp):
        below = ref[x, r0 - 1 : r0 - 1 + rows, :]
        above = ref[x, r0 + 1 : r0 + 1 + rows, :]
        return jnp.where(zp == (x + colour) % 2, below, above)

    def neighbours(ref, x, r0, rows, colour, z):
        centre = ref[x, r0 : r0 + rows, :]
        along_x = ref[x - 1, r0 : r0 + rows, :] + ref[x + 1, r0 : r0 + rows, :]
        return along_x + (centre + sides(ref, x, r0, rows, colour, z % 2)) + lane_sum(centre, 1, z)

    z = lanes(NK)
    zp = z % 2
    row = rows_of(NK)
    whole = slice(PAD, PAD + NK)
    for x in range(NX):
        centre = field(1, x)
        before = field(1, x - 1) if x > 0 else seg0[EXTRA]
        after = field(1, x + 1) if x < NX - 1 else seg3[EXTRA]
        below = jnp.where(row == 0, 0.0, pltpu.roll(centre, 1, 0))
        above = jnp.where(row == NK - 1, 0.0, pltpu.roll(centre, NK - 1, 0))
        side = jnp.where(zp == x % 2, below, above)
        total = (before + after) + (centre + side) + lane_sum(centre, 1, z)
        on = segments[x // H][FLAGS] > 0.5
        red[x, whole, :] = jnp.where(on, (right_side(0, x) + total) * SIXTH, field(0, x))
    for step in range(1, 4):
        colour = step % 2
        dst, src = (red, black) if colour == 0 else (black, red)
        if step == 1:
            for x in (0, NX - 1):
                black[x, whole, :] = field(1, x)
        for x in range(step, NX - step):
            on = segments[x // H][FLAGS] > 0.5
            old = field(1, x) if step == 1 else dst[x, whole, :]
            total = neighbours(src, x, PAD, NK, colour, z)
            dst[x, whole, :] = jnp.where(on, (right_side(colour, x) + total) * SIXTH, old)

    for cx in range(2, NC - 2):
        x = 2 * cx
        u = [red[x + d, whole, :] + black[x + d, whole, :] for d in (-1, 0, 1, 2)]
        w = u[1] + u[2]
        s = (field(2, x) + field(3, x)) + (field(2, x + 1) + field(3, x + 1)) - 4.0 * mean
        total = s - 4.0 * w + (u[0] + u[3]) + lane_sum(w, 1, z)
        for j in range(2):
            total = total + sides(black, x + j, PAD, NK, 0, zp) + sides(red, x + j, PAD, NK, 1, zp)
        coarse[cx] = total * 0.5

    global_row = place[1] * K + row - KH
    row_gain = jnp.where((global_row >= 0) & (global_row < place[3] * K), SIXTH, 0.0).astype(F32)
    parity = (row + z // 2) % 2

    def gain_at(cx):
        if KH <= cx < KH + N // 2:
            return row_gain
        at = place[0] * K + cx - KH
        return row_gain * jnp.where((at >= 0) & (at < place[2] * K), 1.0, 0.0).astype(F32)

    for cx in range(2, NC - 2):
        total = coarse[cx]
        pair = jnp.where(zp == 0, pltpu.roll(total, NZ - 1, 1), pltpu.roll(total, 1, 1))
        total = total + pair
        coarse[cx] = total
        corr[cx, whole, :] = jnp.where(parity == cx % 2, total * gain_at(cx), 0.0)
    for step in range(1, 4):
        for cx in range(2 + step, NC - 2 - step):
            centre = corr[cx, whole, :]
            along_y = corr[cx, PAD - 1 : PAD - 1 + NK, :] + corr[cx, PAD + 1 : PAD + 1 + NK, :]
            along_x = corr[cx - 1, whole, :] + corr[cx + 1, whole, :]
            update = (coarse[cx] + (along_x + along_y) + lane_sum(centre, 2, z)) * gain_at(cx)
            corr[cx, whole, :] = jnp.where(parity == (step + cx) % 2, update, centre)

    rows = slice(PAD + 4, PAD + NK - 4)
    for cx in range(5, NC - 5):
        add = corr[cx, rows, :]
        for ref in (red, black):
            for x in (2 * cx, 2 * cx + 1):
                ref[x, rows, :] = ref[x, rows, :] + add

    z2 = lanes(NK - 8)
    for step in range(4):
        colour = step % 2
        dst, src = (red, black) if colour == 0 else (black, red)
        for x in range(12 + step, NX - 12 - step):
            on = segments[x // H][FLAGS, 4 : NK - 4, :] > 0.5
            total = neighbours(src, x, PAD + 4, NK - 8, colour, z2)
            update = (right_side(colour, x, slice(4, NK - 4)) + total) * SIXTH
            dst[x, rows, :] = jnp.where(on, update, dst[x, rows, :])

    zk = lanes(K)
    r0 = PAD + KH
    own = slice(KH, KH + K)
    for x in range(H, H + N):
        here = zk % 2 == x % 2
        r = red[x, r0 : r0 + K, :]
        b = black[x, r0 : r0 + K, :]
        res_r = right_side(0, x, own) - 6.0 * r + neighbours(black, x, r0, K, 0, zk)
        res_b = right_side(1, x, own) - 6.0 * b + neighbours(red, x, r0, K, 1, zk)
        for ref, one, two in ((smoothed, r, b), (residual, res_r, res_b)):
            ref[x - H, pl.ds(0, K, stride=2), :] = jnp.where(here, one, two)
            ref[x - H, pl.ds(1, K, stride=2), :] = jnp.where(here, two, one)


def shape(*dims):
    return jax.ShapeDtypeStruct(dims, F32)


VMEM = pl.BlockSpec(memory_space=pltpu.VMEM)
SMEM = pl.BlockSpec(memory_space=pltpu.SMEM)
ANY = pl.BlockSpec(memory_space=pltpu.HBM)


def call(kernel, ins, outs, mib, bytes_moved, scratch=()):
    return pl.pallas_call(
        kernel,
        out_shape=outs,
        in_specs=ins,
        out_specs=[VMEM] * len(outs),
        scratch_shapes=list(scratch),
        cost_estimate=pl.CostEstimate(flops=0, bytes_accessed=bytes_moved * MIB, transcendentals=0),
        compiler_params=pltpu.CompilerParams(vmem_limit_bytes=mib * MIB),
    )


def build_pack(groups):
    side = shape(4 * N + 1, KH, NZ)
    return call(
        pack_kernel,
        [ANY, ANY, ANY],
        [side, side, shape(groups, NZ), shape(KH, NZ)],
        56,
        4,
        [
            pltpu.VMEM((N, N, NZ), F32),
            pltpu.VMEM((N, N, NZ), F32),
            pltpu.SMEM((1, 1, NZ // N), jnp.int32),
            pltpu.SemaphoreType.DMA((2 * CHUNKS + 1,)),
        ],
    )


def build_middle(members):
    half = shape(SEGMENT, NK, NZ)
    return call(
        middle_kernel,
        [VMEM, VMEM, ANY, VMEM, VMEM, VMEM],
        [half, half, shape(members, NZ)],
        8,
        6,
        [pltpu.VMEM((KH, NZ), F32), pltpu.SemaphoreType.DMA],
    )


def build_cycle():
    padded = pltpu.VMEM((NX, NK + 2 * PAD, NZ), F32)
    return call(
        cycle_kernel,
        [VMEM] * 5 + [SMEM],
        [shape(N, N, NZ), shape(N, N, NZ)],
        16,
        20,
        [padded, padded, pltpu.VMEM((NC, NK, NZ), F32), pltpu.VMEM((NC, NK + 2 * PAD, NZ), F32)],
    )


def per_device(source, potential, refined):
    groups, members = lax.axis_size(GROUP), lax.axis_size(MEMBER)

    def both_ways(up, down, axis):
        size = lax.axis_size(axis)
        pairs = [(i, i + 1) for i in range(size - 1)]
        return lax.ppermute(up, axis, pairs), lax.ppermute(down, axis, [(b, a) for a, b in pairs])

    up, down, part, flags = build_pack(groups)(source, potential, refined)
    low, high = both_ways(up, down, MEMBER)
    parts = lax.all_to_all(part, GROUP, 0, 0, tiled=True)
    first_half, second_half, part = build_middle(members)(source, potential, flags, low, high, parts)
    before, after = both_ways(second_half, first_half, GROUP)
    parts = lax.all_to_all(part, MEMBER, 0, 0, tiled=True)
    place = jnp.stack(
        [lax.axis_index(GROUP), lax.axis_index(MEMBER), jnp.int32(groups), jnp.int32(members)]
    ).astype(jnp.int32)
    return build_cycle()(before, first_half, second_half, after, parts, place)


def solution(mesh):
    spec = P(GROUP, MEMBER, None)
    return jax.shard_map(
        per_device, mesh=mesh, in_specs=(spec, spec, spec), out_specs=(spec, spec), check_vma=False
    )
```

```python
import functools

import jax
import jax.numpy as jnp
from jax import lax
from jax.experimental import pallas as pl
from jax.experimental.pallas import tpu as pltpu
from jax.sharding import PartitionSpec as P

GROUP = "group"
MEMBER = "member"
N = 32
NZ = 128
K = N // 2
H = 16
KH = H // 2
NX = N + 2 * H
NK = K + 2 * KH
NC = NX // 2
PAD = 8
SIXTH = 1.0 / 6.0
F32 = jnp.float32
MIB = 1024 * 1024
CHUNKS = 1
EXTRA, FLAGS = 4 * H, 4 * H + 1
SEGMENT = 4 * H + 2


def lanes(rows):
    return lax.broadcasted_iota(jnp.int32, (rows, NZ), 1)


def rows_of(rows):
    return lax.broadcasted_iota(jnp.int32, (rows, NZ), 0)


def split(ref, x, first):
    even = ref[x, pl.ds(0, K, stride=2), :]
    odd = ref[x, pl.ds(1, K, stride=2), :]
    return jnp.where(first, even, odd), jnp.where(first, odd, even)


def pack_kernel(source_any, potential_any, refined_any, up, down, part, source, potential, refined, sems):
    size = N // CHUNKS
    flag_copy = pltpu.make_async_copy(refined_any, refined, sems.at[2 * CHUNKS])
    flag_copy.start()
    copies = []
    for c in range(CHUNKS):
        planes = pl.ds(c * size, size)
        pair = []
        for a, (src, dst) in enumerate(((source_any, source), (potential_any, potential))):
            pair.append(pltpu.make_async_copy(src.at[planes], dst.at[planes], sems.at[2 * c + a]))
        for copy in pair:
            copy.start()
        copies.append(pair)
    zp = lanes(K) % 2
    row = rows_of(KH)
    zp8 = lanes(KH) % 2
    acc = [jnp.zeros((K, NZ), F32), jnp.zeros((K, NZ), F32)]
    for x in range(N):
        if x % size == 0:
            for copy in copies[x // size]:
                copy.wait()
        j = x % 2
        first = zp == j
        pr, pb = split(potential, x, first)
        sr, sb = split(source, x, first)
        acc[j] = acc[j] + (sr + sb)
        up[x] = pr[KH:]
        down[x] = pr[:KH]
        up[N + x] = pb[KH:]
        down[N + x] = pb[:KH]
        beyond_up = jnp.where((row == 0) & (zp8 == j), pltpu.roll(pb[:KH], 1, 0), 0.0)
        beyond_down = jnp.where((row == KH - 1) & (zp8 != j), pltpu.roll(pb[KH:], KH - 1, 0), 0.0)
        up[2 * N + x] = sr[KH:] + beyond_up
        down[2 * N + x] = sr[:KH] + beyond_down
        up[3 * N + x] = sb[KH:]
        down[3 * N + x] = sb[:KH]
    total = jnp.sum(acc[0] + acc[1], axis=0, keepdims=True)
    flag_copy.wait()
    box = lanes(KH) // N
    flags = jnp.zeros((KH, NZ), F32)
    for b in range(NZ // N):
        on = jnp.where(refined[0, 0, b] == 1, 1.0, 0.0).astype(F32)
        flags = jnp.where(box == b, on, flags)
    for ref in (up, down):
        ref[4 * N] = flags
    part[...] = jnp.where(rows_of(part.shape[0]) % 2 == 0, total, flags[:1])


def middle_kernel(source, potential, low, high, parts, first_half, second_half, part):
    row = rows_of(parts.shape[0])
    mine = jnp.where(row == 2 * lax.axis_index(GROUP) + 1, parts[...], 0.0)
    own = jnp.broadcast_to(jnp.sum(mine, axis=0, keepdims=True), (KH, NZ))
    totals = jnp.where(row % 2 == 0, parts[...], 0.0)
    part[...] = jnp.broadcast_to(jnp.sum(totals, axis=0, keepdims=True), part.shape)
    zp = lanes(K) % 2
    for x in range(N):
        ref, at = (first_half, x) if x < H else (second_half, x - H)
        here = zp == x % 2
        fields = split(potential, x, here) + split(source, x, here)
        for a in range(4):
            ref[a * H + at, :KH] = low[a * N + x]
            ref[a * H + at, KH : KH + K] = fields[a]
            ref[a * H + at, KH + K :] = high[a * N + x]
            if a == 1 and x in (H - 1, H):
                far = second_half if x == H - 1 else first_half
                far[EXTRA, :KH] = low[a * N + x]
                far[EXTRA, KH : KH + K] = fields[a]
                far[EXTRA, KH + K :] = high[a * N + x]
    for ref in (first_half, second_half):
        ref[FLAGS, :KH] = low[4 * N]
        ref[FLAGS, KH : 2 * KH] = own
        ref[FLAGS, 2 * KH : 3 * KH] = own
        ref[FLAGS, 3 * KH :] = high[4 * N]


def lane_sum(values, step, z):
    left = jnp.where(z < step, 0.0, pltpu.roll(values, step, 1))
    right = jnp.where(z >= NZ - step, 0.0, pltpu.roll(values, NZ - step, 1))
    return left + right


def cycle_kernel(
    cells, seg0, seg1, seg2, seg3_any, parts, place, smoothed, residual, red, black, coarse, corr, seg3, sem
):
    load = pltpu.make_async_copy(seg3_any, seg3, sem)
    load.start()
    segments = (seg0, seg1, seg2, seg3)
    total = jnp.sum(jnp.sum(parts[...], axis=0, keepdims=True), axis=1, keepdims=True)
    mean = total * (1.0 / cells)

    def field(a, x, rows=slice(None)):
        return segments[x // H][a * H + x % H, rows, :]

    def right_side(colour, x, rows=slice(None)):
        return field(2 + colour, x, rows) - mean

    def sides(ref, x, r0, rows, colour, zp):
        below = ref[x, r0 - 1 : r0 - 1 + rows, :]
        above = ref[x, r0 + 1 : r0 + 1 + rows, :]
        return jnp.where(zp == (x + colour) % 2, below, above)

    def neighbours(ref, x, r0, rows, colour, z):
        centre = ref[x, r0 : r0 + rows, :]
        along_x = ref[x - 1, r0 : r0 + rows, :] + ref[x + 1, r0 : r0 + rows, :]
        return along_x + (centre + sides(ref, x, r0, rows, colour, z % 2)) + lane_sum(centre, 1, z)

    z = lanes(NK)
    zp = z % 2
    row = rows_of(NK)
    whole = slice(PAD, PAD + NK)
    for x in range(NX):
        if x + 1 == 3 * H:
            load.wait()
        centre = field(1, x)
        before = field(1, x - 1) if x > 0 else seg0[EXTRA]
        after = field(1, x + 1) if x < NX - 1 else seg3[EXTRA]
        below = jnp.where(row == 0, 0.0, pltpu.roll(centre, 1, 0))
        above = jnp.where(row == NK - 1, 0.0, pltpu.roll(centre, NK - 1, 0))
        side = jnp.where(zp == x % 2, below, above)
        total = (before + after) + (centre + side) + lane_sum(centre, 1, z)
        on = segments[x // H][FLAGS] > 0.5
        red[x, whole, :] = jnp.where(on, (right_side(0, x) + total) * SIXTH, field(0, x))
    for step in range(1, 4):
        colour = step % 2
        dst, src = (red, black) if colour == 0 else (black, red)
        if step == 1:
            for x in (0, NX - 1):
                black[x, whole, :] = field(1, x)
        for x in range(step, NX - step):
            on = segments[x // H][FLAGS] > 0.5
            old = field(1, x) if step == 1 else dst[x, whole, :]
            total = neighbours(src, x, PAD, NK, colour, z)
            dst[x, whole, :] = jnp.where(on, (right_side(colour, x) + total) * SIXTH, old)

    for cx in range(2, NC - 2):
        x = 2 * cx
        u = [red[x + d, whole, :] + black[x + d, whole, :] for d in (-1, 0, 1, 2)]
        w = u[1] + u[2]
        s = (field(2, x) + field(3, x)) + (field(2, x + 1) + field(3, x + 1)) - 4.0 * mean
        total = s - 4.0 * w + (u[0] + u[3]) + lane_sum(w, 1, z)
        for j in range(2):
            total = total + sides(black, x + j, PAD, NK, 0, zp) + sides(red, x + j, PAD, NK, 1, zp)
        coarse[cx] = total * 0.5

    global_row = place[1] * K + row - KH
    row_gain = jnp.where((global_row >= 0) & (global_row < place[3] * K), SIXTH, 0.0).astype(F32)
    parity = (row + z // 2) % 2

    def gain_at(cx):
        if KH <= cx < KH + N // 2:
            return row_gain
        at = place[0] * K + cx - KH
        return row_gain * jnp.where((at >= 0) & (at < place[2] * K), 1.0, 0.0).astype(F32)

    for cx in range(2, NC - 2):
        total = coarse[cx]
        pair = jnp.where(zp == 0, pltpu.roll(total, NZ - 1, 1), pltpu.roll(total, 1, 1))
        total = total + pair
        coarse[cx] = total
        corr[cx, whole, :] = jnp.where(parity == cx % 2, total * gain_at(cx), 0.0)
    for step in range(1, 4):
        for cx in range(2 + step, NC - 2 - step):
            centre = corr[cx, whole, :]
            along_y = corr[cx, PAD - 1 : PAD - 1 + NK, :] + corr[cx, PAD + 1 : PAD + 1 + NK, :]
            along_x = corr[cx - 1, whole, :] + corr[cx + 1, whole, :]
            update = (coarse[cx] + (along_x + along_y) + lane_sum(centre, 2, z)) * gain_at(cx)
            corr[cx, whole, :] = jnp.where(parity == (step + cx) % 2, update, centre)

    rows = slice(PAD + 4, PAD + NK - 4)
    for cx in range(5, NC - 5):
        add = corr[cx, rows, :]
        for ref in (red, black):
            for x in (2 * cx, 2 * cx + 1):
                ref[x, rows, :] = ref[x, rows, :] + add

    z2 = lanes(NK - 8)
    for step in range(4):
        colour = step % 2
        dst, src = (red, black) if colour == 0 else (black, red)
        for x in range(12 + step, NX - 12 - step):
            on = segments[x // H][FLAGS, 4 : NK - 4, :] > 0.5
            total = neighbours(src, x, PAD + 4, NK - 8, colour, z2)
            update = (right_side(colour, x, slice(4, NK - 4)) + total) * SIXTH
            dst[x, rows, :] = jnp.where(on, update, dst[x, rows, :])

    zk = lanes(K)
    r0 = PAD + KH
    own = slice(KH, KH + K)
    for x in range(H, H + N):
        here = zk % 2 == x % 2
        r = red[x, r0 : r0 + K, :]
        b = black[x, r0 : r0 + K, :]
        res_r = right_side(0, x, own) - 6.0 * r + neighbours(black, x, r0, K, 0, zk)
        res_b = right_side(1, x, own) - 6.0 * b + neighbours(red, x, r0, K, 1, zk)
        for ref, one, two in ((smoothed, r, b), (residual, res_r, res_b)):
            ref[x - H, pl.ds(0, K, stride=2), :] = jnp.where(here, one, two)
            ref[x - H, pl.ds(1, K, stride=2), :] = jnp.where(here, two, one)


def shape(*dims):
    return jax.ShapeDtypeStruct(dims, F32)


VMEM = pl.BlockSpec(memory_space=pltpu.VMEM)
SMEM = pl.BlockSpec(memory_space=pltpu.SMEM)
ANY = pl.BlockSpec(memory_space=pltpu.HBM)


def call(kernel, ins, outs, mib, bytes_moved, scratch=()):
    return pl.pallas_call(
        kernel,
        out_shape=outs,
        in_specs=ins,
        out_specs=[VMEM] * len(outs),
        scratch_shapes=list(scratch),
        cost_estimate=pl.CostEstimate(flops=0, bytes_accessed=bytes_moved * MIB, transcendentals=0),
        compiler_params=pltpu.CompilerParams(vmem_limit_bytes=mib * MIB),
    )


def build_pack(groups):
    side = shape(4 * N + 1, KH, NZ)
    return call(
        pack_kernel,
        [ANY, ANY, ANY],
        [side, side, shape(2 * groups, NZ)],
        56,
        4,
        [
            pltpu.VMEM((N, N, NZ), F32),
            pltpu.VMEM((N, N, NZ), F32),
            pltpu.SMEM((1, 1, NZ // N), jnp.int32),
            pltpu.SemaphoreType.DMA((2 * CHUNKS + 1,)),
        ],
    )


def build_middle(members):
    half = shape(SEGMENT, NK, NZ)
    return call(
        middle_kernel,
        [VMEM] * 5,
        [half, half, shape(members, NZ)],
        8,
        6,
    )


def build_cycle(cells):
    padded = pltpu.VMEM((NX, NK + 2 * PAD, NZ), F32)
    return call(
        functools.partial(cycle_kernel, cells),
        [VMEM, VMEM, VMEM, ANY, VMEM, SMEM],
        [shape(N, N, NZ), shape(N, N, NZ)],
        9,
        20,
        [
            padded,
            padded,
            pltpu.VMEM((NC, NK, NZ), F32),
            pltpu.VMEM((NC, NK + 2 * PAD, NZ), F32),
            pltpu.VMEM((SEGMENT, NK, NZ), F32),
            pltpu.SemaphoreType.DMA,
        ],
    )


def per_device(source, potential, refined):
    groups, members = lax.axis_size(GROUP), lax.axis_size(MEMBER)

    def both_ways(up, down, axis):
        size = lax.axis_size(axis)
        pairs = [(i, i + 1) for i in range(size - 1)]
        return lax.ppermute(up, axis, pairs), lax.ppermute(down, axis, [(b, a) for a, b in pairs])

    up, down, part = build_pack(groups)(source, potential, refined)
    low, high = both_ways(up, down, MEMBER)
    parts = lax.all_to_all(part, GROUP, 0, 0, tiled=True)
    first_half, second_half, part = build_middle(members)(source, potential, low, high, parts)
    before, after = both_ways(second_half, first_half, GROUP)
    parts = lax.all_to_all(part, MEMBER, 0, 0, tiled=True)
    place = jnp.stack(
        [lax.axis_index(GROUP), lax.axis_index(MEMBER), jnp.int32(groups), jnp.int32(members)]
    ).astype(jnp.int32)
    return build_cycle(groups * members * N * N * NZ)(before, first_half, second_half, after, parts, place)


def solution(mesh):
    spec = P(GROUP, MEMBER, None)
    return jax.shard_map(
        per_device, mesh=mesh, in_specs=(spec, spec, spec), out_specs=(spec, spec), check_vma=False
    )
```

```python
import functools

import jax
import jax.numpy as jnp
from jax import lax
from jax.experimental import pallas as pl
from jax.experimental.pallas import tpu as pltpu
from jax.sharding import PartitionSpec as P

GROUP = "group"
MEMBER = "member"
N = 32
NZ = 128
K = N // 2
H = 16
KH = H // 2
NX = N + 2 * H
NK = K + 2 * KH
NC = NX // 2
PAD = 8
SIXTH = 1.0 / 6.0
F32 = jnp.float32
MIB = 1024 * 1024
CHUNKS = 1
EXTRA, FLAGS = 4 * H, 4 * H + 1
SEGMENT = 4 * H + 2


def lanes(rows):
    return lax.broadcasted_iota(jnp.int32, (rows, NZ), 1)


def rows_of(rows):
    return lax.broadcasted_iota(jnp.int32, (rows, NZ), 0)


def split(ref, x, first):
    even = ref[x, pl.ds(0, K, stride=2), :]
    odd = ref[x, pl.ds(1, K, stride=2), :]
    return jnp.where(first, even, odd), jnp.where(first, odd, even)


def pack_kernel(source_any, potential_any, refined_any, up, down, part, source, potential, refined, sems):
    size = N // CHUNKS
    flag_copy = pltpu.make_async_copy(refined_any, refined, sems.at[2 * CHUNKS])
    flag_copy.start()
    copies = []
    for c in range(CHUNKS):
        planes = pl.ds(c * size, size)
        pair = []
        for a, (src, dst) in enumerate(((source_any, source), (potential_any, potential))):
            pair.append(pltpu.make_async_copy(src.at[planes], dst.at[planes], sems.at[2 * c + a]))
        for copy in pair:
            copy.start()
        copies.append(pair)
    zp = lanes(K) % 2
    row = rows_of(KH)
    zp8 = lanes(KH) % 2
    acc = [jnp.zeros((K, NZ), F32), jnp.zeros((K, NZ), F32)]
    for x in range(N):
        if x % size == 0:
            for copy in copies[x // size]:
                copy.wait()
        j = x % 2
        first = zp == j
        pr, pb = split(potential, x, first)
        sr, sb = split(source, x, first)
        acc[j] = acc[j] + (sr + sb)
        up[x] = pr[KH:]
        down[x] = pr[:KH]
        up[N + x] = pb[KH:]
        down[N + x] = pb[:KH]
        beyond_up = jnp.where((row == 0) & (zp8 == j), pltpu.roll(pb[:KH], 1, 0), 0.0)
        beyond_down = jnp.where((row == KH - 1) & (zp8 != j), pltpu.roll(pb[KH:], KH - 1, 0), 0.0)
        up[2 * N + x] = sr[KH:] + beyond_up
        down[2 * N + x] = sr[:KH] + beyond_down
        up[3 * N + x] = sb[KH:]
        down[3 * N + x] = sb[:KH]
    total = jnp.sum(acc[0] + acc[1], axis=0, keepdims=True)
    flag_copy.wait()
    box = lanes(KH) // N
    flags = jnp.zeros((KH, NZ), F32)
    for b in range(NZ // N):
        on = jnp.where(refined[0, 0, b] == 1, 1.0, 0.0).astype(F32)
        flags = jnp.where(box == b, on, flags)
    for ref in (up, down):
        ref[4 * N] = flags
    part[...] = jnp.where(rows_of(part.shape[0]) % 2 == 0, total, flags[:1])


def middle_kernel(source, potential, low, high, parts, across, beyond, part):
    even = lax.axis_index(GROUP) % 2 == 0

    @pl.when(even)
    def _():
        middle(source, potential, low, high, parts, beyond, across, part)

    @pl.when(jnp.logical_not(even))
    def _():
        middle(source, potential, low, high, parts, across, beyond, part)


def middle(source, potential, low, high, parts, first_half, second_half, part):
    row = rows_of(parts.shape[0])
    mine = jnp.where(row == 2 * lax.axis_index(GROUP) + 1, parts[...], 0.0)
    own = jnp.broadcast_to(jnp.sum(mine, axis=0, keepdims=True), (KH, NZ))
    totals = jnp.where(row % 2 == 0, parts[...], 0.0)
    part[...] = jnp.broadcast_to(jnp.sum(totals, axis=0, keepdims=True), part.shape)
    zp = lanes(K) % 2
    for x in range(N):
        ref, at = (first_half, x) if x < H else (second_half, x - H)
        here = zp == x % 2
        fields = split(potential, x, here) + split(source, x, here)
        for a in range(4):
            ref[a * H + at, :KH] = low[a * N + x]
            ref[a * H + at, KH : KH + K] = fields[a]
            ref[a * H + at, KH + K :] = high[a * N + x]
            if a == 1 and x in (H - 1, H):
                far = second_half if x == H - 1 else first_half
                far[EXTRA, :KH] = low[a * N + x]
                far[EXTRA, KH : KH + K] = fields[a]
                far[EXTRA, KH + K :] = high[a * N + x]
    for ref in (first_half, second_half):
        ref[FLAGS, :KH] = low[4 * N]
        ref[FLAGS, KH : 2 * KH] = own
        ref[FLAGS, 2 * KH : 3 * KH] = own
        ref[FLAGS, 3 * KH :] = high[4 * N]


def lane_sum(values, step, z):
    left = jnp.where(z < step, 0.0, pltpu.roll(values, step, 1))
    right = jnp.where(z >= NZ - step, 0.0, pltpu.roll(values, NZ - step, 1))
    return left + right


def cycle_kernel(cells, from_across, across, beyond, from_beyond, parts, place, *refs):
    even = place[0] % 2 == 0

    @pl.when(even)
    def _():
        cycle(cells, from_beyond, beyond, across, from_across, parts, place, *refs)

    @pl.when(jnp.logical_not(even))
    def _():
        cycle(cells, from_across, across, beyond, from_beyond, parts, place, *refs)


def cycle(cells, seg0, seg1, seg2, seg3, parts, place, smoothed, residual, red, black, coarse, corr):
    segments = (seg0, seg1, seg2, seg3)
    total = jnp.sum(jnp.sum(parts[...], axis=0, keepdims=True), axis=1, keepdims=True)
    mean = total * (1.0 / cells)

    def field(a, x, rows=slice(None)):
        return segments[x // H][a * H + x % H, rows, :]

    def right_side(colour, x, rows=slice(None)):
        return field(2 + colour, x, rows) - mean

    def sides(ref, x, r0, rows, colour, zp):
        below = ref[x, r0 - 1 : r0 - 1 + rows, :]
        above = ref[x, r0 + 1 : r0 + 1 + rows, :]
        return jnp.where(zp == (x + colour) % 2, below, above)

    def neighbours(ref, x, r0, rows, colour, z):
        centre = ref[x, r0 : r0 + rows, :]
        along_x = ref[x - 1, r0 : r0 + rows, :] + ref[x + 1, r0 : r0 + rows, :]
        return along_x + (centre + sides(ref, x, r0, rows, colour, z % 2)) + lane_sum(centre, 1, z)

    z = lanes(NK)
    zp = z % 2
    row = rows_of(NK)
    whole = slice(PAD, PAD + NK)
    for x in range(NX):
        centre = field(1, x)
        before = field(1, x - 1) if x > 0 else seg0[EXTRA]
        after = field(1, x + 1) if x < NX - 1 else seg3[EXTRA]
        below = jnp.where(row == 0, 0.0, pltpu.roll(centre, 1, 0))
        above = jnp.where(row == NK - 1, 0.0, pltpu.roll(centre, NK - 1, 0))
        side = jnp.where(zp == x % 2, below, above)
        total = (before + after) + (centre + side) + lane_sum(centre, 1, z)
        on = segments[x // H][FLAGS] > 0.5
        red[x, whole, :] = jnp.where(on, (right_side(0, x) + total) * SIXTH, field(0, x))
    for step in range(1, 4):
        colour = step % 2
        dst, src = (red, black) if colour == 0 else (black, red)
        if step == 1:
            for x in (0, NX - 1):
                black[x, whole, :] = field(1, x)
        for x in range(step, NX - step):
            on = segments[x // H][FLAGS] > 0.5
            old = field(1, x) if step == 1 else dst[x, whole, :]
            total = neighbours(src, x, PAD, NK, colour, z)
            dst[x, whole, :] = jnp.where(on, (right_side(colour, x) + total) * SIXTH, old)

    for cx in range(2, NC - 2):
        x = 2 * cx
        u = [red[x + d, whole, :] + black[x + d, whole, :] for d in (-1, 0, 1, 2)]
        w = u[1] + u[2]
        s = (field(2, x) + field(3, x)) + (field(2, x + 1) + field(3, x + 1)) - 4.0 * mean
        total = s - 4.0 * w + (u[0] + u[3]) + lane_sum(w, 1, z)
        for j in range(2):
            total = total + sides(black, x + j, PAD, NK, 0, zp) + sides(red, x + j, PAD, NK, 1, zp)
        coarse[cx] = total * 0.5

    global_row = place[1] * K + row - KH
    row_gain = jnp.where((global_row >= 0) & (global_row < place[3] * K), SIXTH, 0.0).astype(F32)
    parity = (row + z // 2) % 2

    def gain_at(cx):
        if KH <= cx < KH + N // 2:
            return row_gain
        at = place[0] * K + cx - KH
        return row_gain * jnp.where((at >= 0) & (at < place[2] * K), 1.0, 0.0).astype(F32)

    for cx in range(2, NC - 2):
        total = coarse[cx]
        pair = jnp.where(zp == 0, pltpu.roll(total, NZ - 1, 1), pltpu.roll(total, 1, 1))
        total = total + pair
        coarse[cx] = total
        corr[cx, whole, :] = jnp.where(parity == cx % 2, total * gain_at(cx), 0.0)
    for step in range(1, 4):
        for cx in range(2 + step, NC - 2 - step):
            centre = corr[cx, whole, :]
            along_y = corr[cx, PAD - 1 : PAD - 1 + NK, :] + corr[cx, PAD + 1 : PAD + 1 + NK, :]
            along_x = corr[cx - 1, whole, :] + corr[cx + 1, whole, :]
            update = (coarse[cx] + (along_x + along_y) + lane_sum(centre, 2, z)) * gain_at(cx)
            corr[cx, whole, :] = jnp.where(parity == (step + cx) % 2, update, centre)

    rows = slice(PAD + 4, PAD + NK - 4)
    for cx in range(5, NC - 5):
        add = corr[cx, rows, :]
        for ref in (red, black):
            for x in (2 * cx, 2 * cx + 1):
                ref[x, rows, :] = ref[x, rows, :] + add

    z2 = lanes(NK - 8)
    for step in range(4):
        colour = step % 2
        dst, src = (red, black) if colour == 0 else (black, red)
        for x in range(12 + step, NX - 12 - step):
            on = segments[x // H][FLAGS, 4 : NK - 4, :] > 0.5
            total = neighbours(src, x, PAD + 4, NK - 8, colour, z2)
            update = (right_side(colour, x, slice(4, NK - 4)) + total) * SIXTH
            dst[x, rows, :] = jnp.where(on, update, dst[x, rows, :])

    zk = lanes(K)
    r0 = PAD + KH
    own = slice(KH, KH + K)
    for x in range(H, H + N):
        here = zk % 2 == x % 2
        r = red[x, r0 : r0 + K, :]
        b = black[x, r0 : r0 + K, :]
        res_r = right_side(0, x, own) - 6.0 * r + neighbours(black, x, r0, K, 0, zk)
        res_b = right_side(1, x, own) - 6.0 * b + neighbours(red, x, r0, K, 1, zk)
        for ref, one, two in ((smoothed, r, b), (residual, res_r, res_b)):
            ref[x - H, pl.ds(0, K, stride=2), :] = jnp.where(here, one, two)
            ref[x - H, pl.ds(1, K, stride=2), :] = jnp.where(here, two, one)


def shape(*dims):
    return jax.ShapeDtypeStruct(dims, F32)


VMEM = pl.BlockSpec(memory_space=pltpu.VMEM)
SMEM = pl.BlockSpec(memory_space=pltpu.SMEM)
ANY = pl.BlockSpec(memory_space=pltpu.HBM)


def call(kernel, ins, outs, mib, bytes_moved, scratch=()):
    return pl.pallas_call(
        kernel,
        out_shape=outs,
        in_specs=ins,
        out_specs=[VMEM] * len(outs),
        scratch_shapes=list(scratch),
        cost_estimate=pl.CostEstimate(flops=0, bytes_accessed=bytes_moved * MIB, transcendentals=0),
        compiler_params=pltpu.CompilerParams(vmem_limit_bytes=mib * MIB),
    )


def build_pack(groups):
    side = shape(4 * N + 1, KH, NZ)
    return call(
        pack_kernel,
        [ANY, ANY, ANY],
        [side, side, shape(2 * groups, NZ)],
        56,
        4,
        [
            pltpu.VMEM((N, N, NZ), F32),
            pltpu.VMEM((N, N, NZ), F32),
            pltpu.SMEM((1, 1, NZ // N), jnp.int32),
            pltpu.SemaphoreType.DMA((2 * CHUNKS + 1,)),
        ],
    )


def build_middle(members):
    half = shape(SEGMENT, NK, NZ)
    return call(
        middle_kernel,
        [VMEM] * 5,
        [half, half, shape(members, NZ)],
        8,
        6,
    )


def build_cycle(cells):
    padded = pltpu.VMEM((NX, NK + 2 * PAD, NZ), F32)
    return call(
        functools.partial(cycle_kernel, cells),
        [VMEM] * 5 + [SMEM],
        [shape(N, N, NZ), shape(N, N, NZ)],
        9,
        20,
        [
            padded,
            padded,
            pltpu.VMEM((NC, NK, NZ), F32),
            pltpu.VMEM((NC, NK + 2 * PAD, NZ), F32),
        ],
    )


def per_device(source, potential, refined):
    groups, members = lax.axis_size(GROUP), lax.axis_size(MEMBER)

    def both_ways(up, down, axis):
        size = lax.axis_size(axis)
        pairs = [(i, i + 1) for i in range(size - 1)]
        return lax.ppermute(up, axis, pairs), lax.ppermute(down, axis, [(b, a) for a, b in pairs])

    up, down, part = build_pack(groups)(source, potential, refined)
    low, high = both_ways(up, down, MEMBER)
    parts = lax.all_to_all(part, GROUP, 0, 0, tiled=True)
    across, beyond, part = build_middle(members)(source, potential, low, high, parts)
    swaps = [[p for i in range(c, groups - 1, 2) for p in ((i, i + 1), (i + 1, i))] for c in range(2)]
    from_across = lax.ppermute(across, GROUP, swaps[0])
    from_beyond = lax.ppermute(beyond, GROUP, swaps[1])
    parts = lax.all_to_all(part, MEMBER, 0, 0, tiled=True)
    place = jnp.stack(
        [lax.axis_index(GROUP), lax.axis_index(MEMBER), jnp.int32(groups), jnp.int32(members)]
    ).astype(jnp.int32)
    return build_cycle(groups * members * N * N * NZ)(from_across, across, beyond, from_beyond, parts, place)


def solution(mesh):
    spec = P(GROUP, MEMBER, None)
    return jax.shard_map(
        per_device, mesh=mesh, in_specs=(spec, spec, spec), out_specs=(spec, spec), check_vma=False
    )
```
